32 devices in a mesh: groups: 2 (over y), rows: 8 (over z, x), cols: 2 (over core).
Axes of the slice: x: 2, y: 2, z: 4, core: 2. Of those that a mesh axis runs over, the one named last changes fastest.
Arguments:
- query_grad: float32 [65536, 4096], P(('groups', 'rows'), 'cols'), parts along dimension 0, may hold values from -6 to 6
- out_basis: float32 [32768, 256], P('rows'), may hold values from -0.03125 to 0.03125
- in_basis: float32 [4096, 4096], P('cols', 'rows'), may hold values from -0.09375 to 0.09375
- eigenvalues: float32 [256, 4096], P(None, 'rows'), may hold values from 0.01 to 64, as said below
Outputs:
- inverse_product: float32 [65536, 4096], P(('groups', 'rows'), 'cols'), parts along dimension 0
The draws below stay inside these ranges and needn't reach their ends.
There are 2 independent parts, one for each index of `groups`. The reference program is written for one: setup_inputs(seed, part) draws one part's arguments, and reference() takes and returns one part's arrays. A program takes and returns all parts, laid end to end along the dimension named above; an argument that names none is the same for every part. Nothing has to cross between parts.
Inputs may be any that keep to these rules, and one draw needn't show every extreme that they name: `eigenvalues`: positive.
All inputs are finite; a program needn't handle non-finite values.
Results may differ from the reference program's by a relative error of at most 0.000062.
Values sent between devices are 32-bit elements; how exact they have to be, the bound alone decides.
A program may use at most 256 MiB of HBM per device.

```python
import math
import jax
import jax.numpy as jnp
from jax import lax

POUT = 32768
PIN = 4096
WIN = 256


def draw_eigenvalues(key, part):
    key = jax.random.fold_in(key, 7)
    row_key, col_key, jitter_key = jax.random.split(key, 3)
    lowest = 0.01
    spread_top = 10.0
    row_scale = jnp.exp(jax.random.uniform(row_key, (WIN, 1), jnp.float32) * math.log(spread_top))
    col_scale = jnp.exp(jax.random.uniform(col_key, (1, PIN), jnp.float32) * math.log(spread_top))
    upward = jnp.exp(math.log(3.0) * jnp.arange(PIN, dtype=jnp.float32)[None, :] / PIN)
    jitter = jnp.exp(jax.random.uniform(jitter_key, (WIN, PIN), jnp.float32) * math.log(2.0))
    return (lowest * row_scale * col_scale * upward * jitter).astype(jnp.float32)


def block_scale(stream_key, extent, pieces, smallest, high):
    def one(dim, parts):
        steps = jax.random.uniform(jax.random.fold_in(jax.random.fold_in(stream_key, 6), dim), (parts,), jnp.float32, smallest / len(pieces), high / len(pieces))
        return jnp.repeat(jnp.exp(steps), extent[dim] // parts).reshape((-1,) + (1,) * (len(extent) - dim - 1))

    gain = one(*pieces[0])
    for cut in pieces[1:]:
        gain = gain * one(*cut)
    return gain


def noise(rng, dims, deviation, bound, pieces=(), held_as=jnp.bfloat16):
    loudness = block_scale(rng, dims, pieces, -0.22, 0.18) if pieces else 1.0
    array = jax.random.normal(rng, dims, jnp.float32) * deviation * loudness
    return jnp.minimum(jnp.maximum(array, -bound), bound).astype(held_as)


def setup_inputs(seed: int = 0, part: int = 0) -> dict:
    seeds = jax.random.split(jax.random.key(seed), 5)
    part_keys = jax.random.split(jax.random.fold_in(seeds[4], part), 5)
    query_grad = noise(part_keys[0], (POUT, PIN), 1.0, 6.0, ((0, 8), (1, 2)), jnp.float32)
    out_basis = noise(seeds[1], (POUT, WIN), POUT ** -0.5, 0.03125, ((0, 8),), jnp.float32)
    in_basis = noise(seeds[2], (PIN, PIN), PIN ** -0.5, 0.09375, ((0, 2), (1, 8)), jnp.float32)
    eigenvalues = draw_eigenvalues(jax.random.fold_in(seeds[4], 71), part)
    return dict(query_grad=query_grad, out_basis=out_basis, in_basis=in_basis, eigenvalues=eigenvalues)


precise = lax.Precision.HIGHEST


def reference(query_grad, out_basis, in_basis, eigenvalues):
    projected = lax.dot_general(out_basis, query_grad, (((0,), (0,)), ((), ())), precision=precise, preferred_element_type=jnp.float32)
    rotated = jnp.dot(projected, in_basis, precision=precise, preferred_element_type=jnp.float32)
    damping = 0.1 * (jnp.sum(eigenvalues) / (WIN * PIN))
    scaled = rotated / (eigenvalues + damping)
    returned = lax.dot_general(scaled, in_basis, (((1,), (1,)), ((), ())), precision=precise, preferred_element_type=jnp.float32)
    return jnp.dot(out_basis, returned, precision=precise, preferred_element_type=jnp.float32)
```

```python
import functools

import jax
import jax.numpy as jnp
from jax import lax
from jax.experimental import pallas as pl
from jax.experimental.pallas import tpu as pltpu
from jax.sharding import PartitionSpec as P

precise = lax.Precision.HIGHEST
MESH = pl.DeviceIdType.MESH
RING = 8
LANES = 128
MIB = 1024 * 1024


def split(x):
    high = x.astype(jnp.bfloat16)
    low = (x - high.astype(jnp.float32)).astype(jnp.bfloat16)
    return high, low


def dot(a, b, contract=((1,), (0,))):
    return lax.dot_general(a, b, (contract, ((), ())), preferred_element_type=jnp.float32)


def ring_kernel(
    count,
    grad,
    out_basis,
    in_basis,
    eigen,
    result,
    grad_buf,
    basis_t_high,
    basis_t_low,
    basis_in,
    eig,
    ring_a,
    ring_b,
    rotated,
    rotated_peer,
    scaled_high,
    scaled_low,
    totals,
    basis_out,
    grad_sem,
    local_sem,
    send_a,
    recv_a,
    send_b,
    recv_b,
    send_t,
    recv_t,
    send_c,
    recv_c,
):
    row = lax.axis_index("rows")
    col = lax.axis_index("cols")
    depth = grad.shape[0]
    slots = grad_buf.shape[0]

    z, x = row // 2, row % 2
    place = z + x * (RING - 1 - 2 * z)

    def row_of(position):
        return 2 * position + (position // 4) * (2 * RING - 1 - 4 * position)

    right = row_of((place + 1) % RING)
    left = row_of((place + RING - 1) % RING)

    def chunk(direction, step):
        turn = (place + 2 * RING - step) if direction == 0 else (place + step)
        return pl.multiple_of((turn % RING) * (2 * LANES) + direction * LANES, LANES)

    def fetch(step, direction):
        return pltpu.make_async_copy(
            grad.at[:, pl.ds(chunk(direction, step), LANES)],
            grad_buf.at[step % slots, direction],
            grad_sem.at[step % slots, direction],
        )

    load_basis = pltpu.make_async_copy(out_basis, basis_out, local_sem.at[0])
    load_eig = pltpu.make_async_copy(eigen, eig, local_sem.at[1])
    load_in = pltpu.make_async_copy(in_basis, basis_in, local_sem.at[2])
    load_basis.start()
    for step in range(slots):
        for direction in range(2):
            fetch(step, direction).start()
        if step == 0:
            load_eig.start()
            load_in.start()

    barrier = pltpu.get_barrier_semaphore()
    for offset in range(1, RING):
        pl.semaphore_signal(
            barrier, inc=1, device_id={"rows": (row + offset) % RING}, device_id_type=MESH
        )
    pl.semaphore_signal(barrier, inc=1, device_id={"cols": 1 - col}, device_id_type=MESH)

    load_basis.wait()
    piece = min(512, depth)
    for start in range(0, depth, piece):
        high, low = split(basis_out[start : start + piece, :].T)
        basis_t_high[:, start : start + piece] = high
        basis_t_low[:, start : start + piece] = low

    load_eig.wait()
    sums = jnp.sum(eig[...], axis=0, keepdims=True)
    lane_sums = sums[:, 0:LANES]
    for start in range(LANES, eig.shape[1], LANES):
        lane_sums = lane_sums + sums[:, start : start + LANES]
    totals[pl.ds(row, 1)] = jnp.broadcast_to(lane_sums, (8, LANES))[None]

    pl.semaphore_wait(barrier, RING)

    def total_copy(offset):
        return pltpu.make_async_remote_copy(
            src_ref=totals.at[row],
            dst_ref=totals.at[row],
            send_sem=send_t.at[offset - 1],
            recv_sem=recv_t.at[offset - 1],
            device_id={"rows": (row + offset) % RING},
            device_id_type=MESH,
        )

    for offset in range(1, RING):
        total_copy(offset).start()

    def hop(ring, send, recv, direction, step):
        return pltpu.make_async_remote_copy(
            src_ref=ring.at[direction, step],
            dst_ref=ring.at[direction, step + 1],
            send_sem=send.at[direction, step],
            recv_sem=recv.at[direction, step],
            device_id={"rows": right if direction == 0 else left},
            device_id_type=MESH,
        )

    def reduce_step(ring, send, recv, step, local):
        @pl.when(step == 0)
        def _():
            for direction in range(2):
                ring[direction, 0] = local[direction]
                hop(ring, send, recv, direction, 0).start()

        @pl.when(step > 0)
        def _():
            for direction in range(2):
                hop(ring, send, recv, direction, step - 1).wait_recv()
                ring[direction, step] = ring[direction, step] + local[direction]
                hop(ring, send, recv, direction, step).start()

    def project(step, carry):
        fetch(step, 0).wait()
        fetch(step, 1).wait()
        slot = step % slots
        local = [None, None]
        block = min(1024, depth)
        for start in range(0, depth, block):
            rows = slice(start, start + block)
            one_high, one_low = split(grad_buf[slot, 0, rows, :])
            two_high, two_low = split(grad_buf[slot, 1, rows, :])
            upper = jnp.concatenate([one_high, one_low, two_high, two_low], axis=1)
            wide = dot(basis_t_high[:, rows], upper)
            highs = jnp.concatenate([one_high, two_high], axis=1)
            narrow = dot(basis_t_low[:, rows], highs)
            for direction in range(2):
                at = 2 * direction * LANES
                term = (
                    wide[:, at : at + LANES]
                    + wide[:, at + LANES : at + 2 * LANES]
                    + narrow[:, direction * LANES : (direction + 1) * LANES]
                )
                local[direction] = term if start == 0 else local[direction] + term

        @pl.when(step + slots < RING)
        def _():
            fetch(step + slots, 0).start()
            fetch(step + slots, 1).start()

        reduce_step(ring_a, send_a, recv_a, step, local)
        return carry

    lax.fori_loop(0, RING, project, 0)

    load_in.wait()
    rotated[...] = jnp.zeros_like(rotated)

    def basis_rows(step):
        return jnp.concatenate(
            [basis_in[pl.ds(chunk(direction, step), LANES), :] for direction in range(2)], axis=0
        )

    def arrive(ring, send, recv, step):
        @pl.when(step >= RING)
        def _():
            for direction in range(2):
                hop(ring, send, recv, direction, step - 1).wait_recv()

                @pl.when(step < 2 * RING - 2)
                def _():
                    hop(ring, send, recv, direction, step).start()

    def rotate(step, carry):
        b_high, b_low = split(basis_rows(step))
        arrive(ring_a, send_a, recv_a, step)
        p_high, p_low = split(jnp.concatenate([ring_a[0, step], ring_a[1, step]], axis=1))
        rotated[...] += dot(
            jnp.concatenate([p_high, p_high, p_low], axis=1),
            jnp.concatenate([b_high, b_low, b_high], axis=0),
        )
        return carry

    lax.fori_loop(RING - 1, 2 * RING - 1, rotate, 0)

    swap = pltpu.make_async_remote_copy(
        src_ref=rotated,
        dst_ref=rotated_peer,
        send_sem=send_c,
        recv_sem=recv_c,
        device_id={"cols": 1 - col},
        device_id_type=MESH,
    )
    swap.start()
    for offset in range(1, RING):
        total_copy(offset).wait()
    overall = jnp.sum(totals[...], axis=0)[0:1, :]
    overall = jnp.sum(overall, axis=1, keepdims=True)
    divisor = eig[...] + 0.1 * (overall / count)
    swap.wait()
    high, low = split((rotated[...] + rotated_peer[...]) / divisor)
    scaled_high[...] = high
    scaled_low[...] = low

    def give_back(step, carry):
        b_high, b_low = split(basis_rows(step))
        s_high, s_low = scaled_high[...], scaled_low[...]
        both = ((1,), (1,))
        part = dot(s_high, b_high, both) + dot(s_high, b_low, both) + dot(s_low, b_high, both)
        reduce_step(ring_b, send_b, recv_b, step, [part[:, :LANES], part[:, LANES:]])
        return carry

    lax.fori_loop(0, RING, give_back, 0)

    def collect(step, carry):
        arrive(ring_b, send_b, recv_b, step)
        for direction in range(2):
            result[:, pl.ds(chunk(direction, step), LANES)] = ring_b[direction, step]
        return carry

    lax.fori_loop(RING - 1, 2 * RING - 1, collect, 0)

    def drain(step, carry):
        for direction in range(2):
            hop(ring_a, send_a, recv_a, direction, step).wait_send()
            hop(ring_b, send_b, recv_b, direction, step).wait_send()
        return carry

    lax.fori_loop(0, 2 * RING - 2, drain, 0)


def back_rotated(query_grad, out_basis, in_basis, eigenvalues, count):
    depth, columns = query_grad.shape
    window = out_basis.shape[1]
    directions = in_basis.shape[1]
    slots = 4
    hops = 2 * RING - 2
    dma = pltpu.SemaphoreType.DMA
    f32, bf16 = jnp.float32, jnp.bfloat16
    flops = 6 * window * columns * (depth + 2 * directions)
    return pl.pallas_call(
        functools.partial(ring_kernel, count),
        out_shape=jax.ShapeDtypeStruct((window, columns), f32),
        in_specs=[pl.BlockSpec(memory_space=pl.ANY)] * 4,
        out_specs=pl.BlockSpec(memory_space=pltpu.VMEM),
        scratch_shapes=[
            pltpu.VMEM((slots, 2, depth, LANES), f32),
            pltpu.VMEM((window, depth), bf16),
            pltpu.VMEM((window, depth), bf16),
            pltpu.VMEM((columns, directions), f32),
            pltpu.VMEM((window, directions), f32),
            pltpu.VMEM((2, hops + 1, window, LANES), f32),
            pltpu.VMEM((2, hops + 1, window, LANES), f32),
            pltpu.VMEM((window, directions), f32),
            pltpu.VMEM((window, directions), f32),
            pltpu.VMEM((window, directions), bf16),
            pltpu.VMEM((window, directions), bf16),
            pltpu.VMEM((RING, 8, LANES), f32),
            pltpu.VMEM((depth, window), f32),
            dma((slots, 2)),
            dma((3,)),
            dma((2, hops)),
            dma((2, hops)),
            dma((2, hops)),
            dma((2, hops)),
            dma((RING - 1,)),
            dma((RING - 1,)),
            dma,
            dma,
        ],
        compiler_params=pltpu.CompilerParams(
            collective_id=0, has_side_effects=True, vmem_limit_bytes=56 * MIB
        ),
        cost_estimate=pl.CostEstimate(
            flops=flops, bytes_accessed=4 * depth * (columns + window), transcendentals=0
        ),
        name="ring_kernel",
    )(query_grad, out_basis, in_basis, eigenvalues)


def expand_kernel(basis, returned, out, stacked):
    @pl.when(pl.program_id(0) == 0)
    def _():
        r_high, r_low = split(returned[...])
        stacked[...] = jnp.concatenate([r_high, r_low, r_high], axis=0)

    u_high, u_low = split(basis[...])
    out[...] = dot(jnp.concatenate([u_high, u_high, u_low], axis=1), stacked[...])


def expand(out_basis, returned):
    depth, window = out_basis.shape
    columns = returned.shape[1]
    tile = min(512, depth)
    return pl.pallas_call(
        expand_kernel,
        grid=(depth // tile,),
        out_shape=jax.ShapeDtypeStruct((depth, columns), jnp.float32),
        in_specs=[
            pl.BlockSpec((tile, window), lambda i: (i, 0)),
            pl.BlockSpec((window, columns), lambda i: (0, 0)),
        ],
        out_specs=pl.BlockSpec((tile, columns), lambda i: (i, 0)),
        scratch_shapes=[pltpu.VMEM((3 * window, columns), jnp.bfloat16)],
        compiler_params=pltpu.CompilerParams(vmem_limit_bytes=40 * MIB),
        cost_estimate=pl.CostEstimate(
            flops=6 * depth * window * columns,
            bytes_accessed=4 * depth * (columns + window),
            transcendentals=0,
        ),
        name="expand_kernel",
    )(out_basis, returned)


def with_collectives(query_grad, out_basis, in_basis, eigenvalues, count):
    def product(a, b, contract):
        return lax.dot_general(
            a, b, (contract, ((), ())), precision=precise, preferred_element_type=jnp.float32
        )

    projected = lax.psum(product(out_basis, query_grad, ((0,), (0,))), "rows")
    damping = 0.1 * (lax.psum(jnp.sum(eigenvalues), "rows") / count)
    rotated = lax.psum(product(projected, in_basis, ((1,), (0,))), "cols")
    scaled = rotated / (eigenvalues + damping)
    return lax.psum(product(scaled, in_basis, ((1,), (1,))), "rows")


def per_device(sizes, query_grad, out_basis, in_basis, eigenvalues):
    rows, cols = sizes
    count = eigenvalues.shape[0] * eigenvalues.shape[1] * rows
    on_ring = (
        rows == RING
        and cols == 2
        and query_grad.shape[1] == 2 * RING * LANES
        and eigenvalues.shape[1] % LANES == 0
    )
    inner = back_rotated if on_ring else with_collectives
    returned = inner(query_grad, out_basis, in_basis, eigenvalues, count)
    return expand(out_basis, returned)


def solution(mesh):
    return jax.shard_map(
        functools.partial(per_device, (mesh.shape["rows"], mesh.shape["cols"])),
        mesh=mesh,
        in_specs=(
            P(("groups", "rows"), "cols"),
            P("rows", None),
            P("cols", "rows"),
            P(None, "rows"),
        ),
        out_specs=P(("groups", "rows"), "cols"),
        check_vma=False,
    )
```

```python
import functools

import jax
import jax.numpy as jnp
from jax import lax
from jax.experimental import pallas as pl
from jax.experimental.pallas import tpu as pltpu
from jax.sharding import PartitionSpec as P

precise = lax.Precision.HIGHEST
MESH = pl.DeviceIdType.MESH
RING = 8
LANES = 128
STREAMS = 2
MIB = 1024 * 1024


def split(x):
    high = x.astype(jnp.bfloat16)
    low = (x - high.astype(jnp.float32)).astype(jnp.bfloat16)
    return high, low


def dot(a, b, contract=((1,), (0,))):
    return lax.dot_general(a, b, (contract, ((), ())), preferred_element_type=jnp.float32)


def ring_kernel(
    count,
    grad,
    out_basis,
    in_basis,
    eigen,
    result,
    grad_buf,
    basis_t_high,
    basis_t_low,
    basis_in,
    eig,
    ring_a,
    ring_b,
    rotated,
    rotated_peer,
    scaled_high,
    scaled_low,
    totals,
    basis_out,
    grad_sem,
    local_sem,
    send_a,
    recv_a,
    send_b,
    recv_b,
    send_t,
    recv_t,
    send_c,
    recv_c,
):
    row = lax.axis_index("rows")
    col = lax.axis_index("cols")
    depth = grad.shape[0]
    slots = grad_buf.shape[0]

    z, x = row // 2, row % 2
    place = z + x * (RING - 1 - 2 * z)

    def row_of(position):
        return 2 * position + (position // 4) * (2 * RING - 1 - 4 * position)

    right = row_of((place + 1) % RING)
    left = row_of((place + RING - 1) % RING)

    half = RING // 2

    def chunk(side, offset):
        turn = place + RING + (offset if side == 0 else -offset)
        return pl.multiple_of((turn % RING) * (2 * LANES) + side * LANES, LANES)

    def toward_owner(step):
        kind, hops = step % 2, step // 2
        return (1 - kind) * (half - hops) + kind * (hops + 1 - half)

    def from_owner(step):
        kind, hops = (step + 1) % 2, (step + 1) // 2
        return (2 * kind - 1) * hops

    def fetch(step, direction):
        return pltpu.make_async_copy(
            grad.at[:, pl.ds(chunk(direction, toward_owner(step)), LANES)],
            grad_buf.at[step % slots, direction],
            grad_sem.at[step % slots, direction],
        )

    load_basis = pltpu.make_async_copy(out_basis, basis_out, local_sem.at[0])
    load_eig = pltpu.make_async_copy(eigen, eig, local_sem.at[1])
    load_in = pltpu.make_async_copy(in_basis, basis_in, local_sem.at[2])
    load_basis.start()
    for step in range(slots):
        for direction in range(2):
            fetch(step, direction).start()
        if step == 0:
            load_eig.start()
            load_in.start()

    barrier = pltpu.get_barrier_semaphore()
    for offset in range(1, RING):
        pl.semaphore_signal(
            barrier, inc=1, device_id={"rows": (row + offset) % RING}, device_id_type=MESH
        )
    pl.semaphore_signal(barrier, inc=1, device_id={"cols": 1 - col}, device_id_type=MESH)

    load_basis.wait()
    piece = min(512, depth)
    for start in range(0, depth, piece):
        high, low = split(basis_out[start : start + piece, :].T)
        basis_t_high[:, start : start + piece] = high
        basis_t_low[:, start : start + piece] = low

    load_eig.wait()
    sums = jnp.sum(eig[...], axis=0, keepdims=True)
    lane_sums = sums[:, 0:LANES]
    for start in range(LANES, eig.shape[1], LANES):
        lane_sums = lane_sums + sums[:, start : start + LANES]
    totals[pl.ds(row, 1)] = jnp.broadcast_to(lane_sums, (8, LANES))[None]

    pl.semaphore_wait(barrier, RING)

    def total_copy(offset):
        return pltpu.make_async_remote_copy(
            src_ref=totals.at[row],
            dst_ref=totals.at[row],
            send_sem=send_t.at[offset - 1],
            recv_sem=recv_t.at[offset - 1],
            device_id={"rows": (row + offset) % RING},
            device_id_type=MESH,
        )

    for offset in range(1, RING):
        total_copy(offset).start()

    def hop(ring, send, recv, kind, side, step, stream):
        back = kind if side == 0 else 1 - kind
        return pltpu.make_async_remote_copy(
            src_ref=ring.at[kind, side, step, stream],
            dst_ref=ring.at[kind, side, step + 1, stream],
            send_sem=send.at[kind, side, step, stream],
            recv_sem=recv.at[kind, side, step, stream],
            device_id={"rows": right + back * (left - right)},
            device_id_type=MESH,
        )

    pieces = [(stream, side) for stream in range(STREAMS) for side in range(2)]
    band = ring_a.shape[4]

    def reduce_step(ring, send, recv, step, local):
        kind, hops = step % 2, step // 2

        def term(stream, side):
            return local[side][stream * band : (stream + 1) * band, :]

        @pl.when(step < 2)
        def _():
            for stream, side in pieces:
                ring[kind, side, 0, stream] = term(stream, side)
                hop(ring, send, recv, kind, side, 0, stream).start()

        @pl.when((step >= 2) & (step < RING - 1))
        def _():
            for stream, side in pieces:
                hop(ring, send, recv, kind, side, hops - 1, stream).wait_recv()
                ring[kind, side, hops, stream] = ring[kind, side, hops, stream] + term(
                    stream, side
                )
                hop(ring, send, recv, kind, side, hops, stream).start()

        @pl.when(step == RING - 1)
        def _():
            for stream, side in pieces:
                hop(ring, send, recv, 0, side, half - 1, stream).wait_recv()
                hop(ring, send, recv, 1, side, half - 2, stream).wait_recv()
                own = (
                    ring[0, side, half, stream]
                    + ring[1, side, half - 1, stream]
                    + term(stream, side)
                )
                for way in range(2):
                    ring[way, side, half, stream] = own
                    hop(ring, send, recv, way, side, half, stream).start()

    def whole(ring, side, step):
        kind, hops = (step + 1) % 2, (step + 1) // 2
        return ring[kind, side, half + hops].reshape(STREAMS * band, LANES)

    def project(step, carry):
        fetch(step, 0).wait()
        fetch(step, 1).wait()
        slot = step % slots
        local = [None, None]
        block = min(1024, depth)
        for start in range(0, depth, block):
            rows = slice(start, start + block)
            one_high, one_low = split(grad_buf[slot, 0, rows, :])
            two_high, two_low = split(grad_buf[slot, 1, rows, :])
            upper = jnp.concatenate([one_high, one_low, two_high, two_low], axis=1)
            wide = dot(basis_t_high[:, rows], upper)
            highs = jnp.concatenate([one_high, two_high], axis=1)
            narrow = dot(basis_t_low[:, rows], highs)
            for direction in range(2):
                at = 2 * direction * LANES
                term = (
                    wide[:, at : at + LANES]
                    + wide[:, at + LANES : at + 2 * LANES]
                    + narrow[:, direction * LANES : (direction + 1) * LANES]
                )
                local[direction] = term if start == 0 else local[direction] + term

        @pl.when(step + slots < RING)
        def _():
            fetch(step + slots, 0).start()
            fetch(step + slots, 1).start()

        reduce_step(ring_a, send_a, recv_a, step, local)
        return carry

    lax.fori_loop(0, RING, project, 0)

    load_in.wait()
    rotated[...] = jnp.zeros_like(rotated)

    def basis_rows(offset):
        return jnp.concatenate(
            [basis_in[pl.ds(chunk(side, offset), LANES), :] for side in range(2)], axis=0
        )

    def arrive(ring, send, recv, step):
        kind, hops = (step + 1) % 2, (step + 1) // 2

        @pl.when(step > 0)
        def _():
            for stream, side in pieces:
                hop(ring, send, recv, kind, side, half + hops - 1, stream).wait_recv()

                @pl.when(hops < half - kind)
                def _():
                    hop(ring, send, recv, kind, side, half + hops, stream).start()

    def rotate(step, carry):
        b_high, b_low = split(basis_rows(from_owner(step)))
        arrive(ring_a, send_a, recv_a, step)
        p_high, p_low = split(jnp.concatenate([whole(ring_a, 0, step), whole(ring_a, 1, step)], axis=1))
        rotated[...] += dot(
            jnp.concatenate([p_high, p_high, p_low], axis=1),
            jnp.concatenate([b_high, b_low, b_high], axis=0),
        )
        return carry

    lax.fori_loop(0, RING, rotate, 0)

    swap = pltpu.make_async_remote_copy(
        src_ref=rotated,
        dst_ref=rotated_peer,
        send_sem=send_c,
        recv_sem=recv_c,
        device_id={"cols": 1 - col},
        device_id_type=MESH,
    )
    swap.start()
    for offset in range(1, RING):
        total_copy(offset).wait()
    overall = jnp.sum(totals[...], axis=0)[0:1, :]
    overall = jnp.sum(overall, axis=1, keepdims=True)
    divisor = eig[...] + 0.1 * (overall / count)
    swap.wait()
    high, low = split((rotated[...] + rotated_peer[...]) / divisor)
    scaled_high[...] = high
    scaled_low[...] = low

    def give_back(step, carry):
        b_high, b_low = split(basis_rows(toward_owner(step)))
        s_high, s_low = scaled_high[...], scaled_low[...]
        both = ((1,), (1,))
        part = dot(s_high, b_high, both) + dot(s_high, b_low, both) + dot(s_low, b_high, both)
        reduce_step(ring_b, send_b, recv_b, step, [part[:, :LANES], part[:, LANES:]])
        return carry

    lax.fori_loop(0, RING, give_back, 0)

    def collect(step, carry):
        arrive(ring_b, send_b, recv_b, step)
        for direction in range(2):
            result[:, pl.ds(chunk(direction, from_owner(step)), LANES)] = whole(ring_b, direction, step)
        return carry

    lax.fori_loop(0, RING, collect, 0)

    def drain(step, carry):
        for stream, side in pieces:
            for ring, send, recv in ((ring_a, send_a, recv_a), (ring_b, send_b, recv_b)):
                hop(ring, send, recv, 0, side, step, stream).wait_send()

                @pl.when((step != half - 1) & (step != RING - 1))
                def _():
                    hop(ring, send, recv, 1, side, step, stream).wait_send()

        return carry

    lax.fori_loop(0, RING, drain, 0)


def back_rotated(query_grad, out_basis, in_basis, eigenvalues, count):
    depth, columns = query_grad.shape
    window = out_basis.shape[1]
    directions = in_basis.shape[1]
    slots = 4
    dma = pltpu.SemaphoreType.DMA
    f32, bf16 = jnp.float32, jnp.bfloat16
    flops = 6 * window * columns * (depth + 2 * directions)
    return pl.pallas_call(
        functools.partial(ring_kernel, count),
        out_shape=jax.ShapeDtypeStruct((window, columns), f32),
        in_specs=[pl.BlockSpec(memory_space=pl.ANY)] * 4,
        out_specs=pl.BlockSpec(memory_space=pltpu.VMEM),
        scratch_shapes=[
            pltpu.VMEM((slots, 2, depth, LANES), f32),
            pltpu.VMEM((window, depth), bf16),
            pltpu.VMEM((window, depth), bf16),
            pltpu.VMEM((columns, directions), f32),
            pltpu.VMEM((window, directions), f32),
            pltpu.VMEM((2, 2, RING + 1, STREAMS, window // STREAMS, LANES), f32),
            pltpu.VMEM((2, 2, RING + 1, STREAMS, window // STREAMS, LANES), f32),
            pltpu.VMEM((window, directions), f32),
            pltpu.VMEM((window, directions), f32),
            pltpu.VMEM((window, directions), bf16),
            pltpu.VMEM((window, directions), bf16),
            pltpu.VMEM((RING, 8, LANES), f32),
            pltpu.VMEM((depth, window), f32),
            dma((slots, 2)),
            dma((3,)),
            dma((2, 2, RING, STREAMS)),
            dma((2, 2, RING, STREAMS)),
            dma((2, 2, RING, STREAMS)),
            dma((2, 2, RING, STREAMS)),
            dma((RING - 1,)),
            dma((RING - 1,)),
            dma,
            dma,
        ],
        compiler_params=pltpu.CompilerParams(
            collective_id=0, has_side_effects=True, vmem_limit_bytes=56 * MIB
        ),
        cost_estimate=pl.CostEstimate(
            flops=flops, bytes_accessed=4 * depth * (columns + window), transcendentals=0
        ),
        name="ring_kernel",
    )(query_grad, out_basis, in_basis, eigenvalues)


def expand_kernel(basis, returned, out, stacked):
    @pl.when(pl.program_id(0) == 0)
    def _():
        r_high, r_low = split(returned[...])
        stacked[...] = jnp.concatenate([r_high, r_low, r_high], axis=0)

    u_high, u_low = split(basis[...])
    out[...] = dot(jnp.concatenate([u_high, u_high, u_low], axis=1), stacked[...])


def expand(out_basis, returned):
    depth, window = out_basis.shape
    columns = returned.shape[1]
    tile = min(256, depth)
    return pl.pallas_call(
        expand_kernel,
        grid=(depth // tile,),
        out_shape=jax.ShapeDtypeStruct((depth, columns), jnp.float32),
        in_specs=[
            pl.BlockSpec((tile, window), lambda i: (i, 0)),
            pl.BlockSpec((window, columns), lambda i: (0, 0)),
        ],
        out_specs=pl.BlockSpec((tile, columns), lambda i: (i, 0)),
        scratch_shapes=[pltpu.VMEM((3 * window, columns), jnp.bfloat16)],
        compiler_params=pltpu.CompilerParams(vmem_limit_bytes=40 * MIB),
        cost_estimate=pl.CostEstimate(
            flops=6 * depth * window * columns,
            bytes_accessed=4 * depth * (columns + window),
            transcendentals=0,
        ),
        name="expand_kernel",
    )(out_basis, returned)


def with_collectives(query_grad, out_basis, in_basis, eigenvalues, count):
    def product(a, b, contract):
        return lax.dot_general(
            a, b, (contract, ((), ())), precision=precise, preferred_element_type=jnp.float32
        )

    projected = lax.psum(product(out_basis, query_grad, ((0,), (0,))), "rows")
    damping = 0.1 * (lax.psum(jnp.sum(eigenvalues), "rows") / count)
    rotated = lax.psum(product(projected, in_basis, ((1,), (0,))), "cols")
    scaled = rotated / (eigenvalues + damping)
    return lax.psum(product(scaled, in_basis, ((1,), (1,))), "rows")


def per_device(sizes, query_grad, out_basis, in_basis, eigenvalues):
    rows, cols = sizes
    count = eigenvalues.shape[0] * eigenvalues.shape[1] * rows
    on_ring = (
        rows == RING
        and cols == 2
        and query_grad.shape[1] == 2 * RING * LANES
        and eigenvalues.shape[1] % LANES == 0
    )
    inner = back_rotated if on_ring else with_collectives
    returned = inner(query_grad, out_basis, in_basis, eigenvalues, count)
    return expand(out_basis, returned)


def solution(mesh):
    return jax.shard_map(
        functools.partial(per_device, (mesh.shape["rows"], mesh.shape["cols"])),
        mesh=mesh,
        in_specs=(
            P(("groups", "rows"), "cols"),
            P("rows", None),
            P("cols", "rows"),
            P(None, "rows"),
        ),
        out_specs=P(("groups", "rows"), "cols"),
        check_vma=False,
    )
```
